32 devices in a mesh: rep: 4 (over y, x), fsdp: 8 (over z, core).
Axes of the slice: x: 2, y: 2, z: 4, core: 2. Of those that a mesh axis runs over, the one named last changes fastest.
Arguments:
- tokens: bfloat16 [16384, 8192], P(('rep', 'fsdp')), may hold values from -6 to 6
- norm_gain: bfloat16 [8192], replicated, may hold values from 0.5 to 1.5
- step_counts: int32 [4], P('rep'), may hold values from 25 to 100
- local_params: bfloat16 [4, 8192, 1024], P('rep', 'fsdp'), may hold values from -6 to 6
- global_params: float32 [8192, 1024], P('fsdp', 'rep'), may hold values from -6 to 6
- momentum: float32 [8192, 1024], P('fsdp', 'rep'), may hold values from -3 to 3
Outputs:
- keys_values: bfloat16 [16384, 1024], P(('rep', 'fsdp'))
- new_local: bfloat16 [4, 8192, 1024], P('rep', 'fsdp')
- new_global: float32 [8192, 1024], P('fsdp', 'rep')
- new_momentum: float32 [8192, 1024], P('fsdp', 'rep')
The draws below stay inside these ranges and needn't reach their ends.
All inputs are finite; a program needn't handle non-finite values.
Results may differ from the reference program's by a relative error of at most 0.0057.
Values may be sent and summed in bfloat16 or wider, within the bound.
A program may use at most 128 MiB of HBM per device.

```python
import jax
import jax.numpy as jnp
from jax import lax

D = 8192
C = 1024
TOK_REP = 4096
TOKENS = 16384
N_REP = 4


def place_ends(values, stream_key, smallest, high):
    shape = values.shape
    place = [jax.random.randint(jax.random.fold_in(stream_key, axis), (), 0, shape[axis]) for axis in range(len(shape))]
    values = values.at[tuple(place)].set(smallest)
    longest = shape.index(max(shape))
    place[longest] = (place[longest] + 1) % shape[longest]
    return values.at[tuple(place)].set(high)


def shard_levels(stream_key, dims, split, least, top_value):
    def one(axis_at, parts):
        draws = jax.random.uniform(jax.random.fold_in(jax.random.fold_in(stream_key, 6), axis_at), (parts,), jnp.float32, least / len(split), top_value / len(split))
        return jnp.repeat(jnp.exp(draws), dims[axis_at] // parts).reshape((-1,) + (1,) * (len(dims) - axis_at - 1))

    loudness = one(*split[0])
    for cut in split[1:]:
        loudness = loudness * one(*cut)
    return loudness


def normal_values(rng, extent, width, reach, pieces=(), held_as=jnp.bfloat16):
    drawn = jax.random.normal(rng, extent, jnp.float32) * width
    if len(pieces) > 0:
        drawn = shard_levels(rng, extent, pieces, -0.22, 0.18) * drawn
    return jnp.clip(drawn, min=-reach, max=reach).astype(held_as)


def setup_inputs(seed: int = 0) -> dict:
    seeds = jax.random.split(jax.random.key(seed), 7)
    tokens = normal_values(seeds[0], (TOKENS, D), 1.0, 6.0, ((0, 32),))
    norm_gain = jnp.clip(1.0 + 0.1 * jax.random.normal(seeds[1], (D,), jnp.float32), 0.5, 1.5).astype(jnp.bfloat16)
    step_counts = place_ends(jax.random.randint(seeds[2], (N_REP,), 25, 101), jax.random.fold_in(seeds[2], 1), 25, 100).astype(jnp.int32)
    local_params = normal_values(seeds[3], (N_REP, D, C), 1.0, 6.0, ((0, 4), (1, 8)))
    global_params = normal_values(seeds[4], (D, C), 1.0, 6.0, ((0, 8), (1, 4)), jnp.float32)
    momentum = normal_values(seeds[5], (D, C), 0.5, 3.0, ((0, 8), (1, 4)), jnp.float32)
    return dict(tokens=tokens, norm_gain=norm_gain, step_counts=step_counts, local_params=local_params, global_params=global_params, momentum=momentum)


def reference(tokens, norm_gain, step_counts, local_params, global_params, momentum):
    counts = step_counts.astype(jnp.float32)
    total = jnp.sum(counts)
    weighted = lax.optimization_barrier(jnp.sum(counts[:, None, None] * local_params.astype(jnp.float32), axis=0))
    delta = global_params - weighted / total
    new_momentum = 0.9 * momentum + delta
    new_global = global_params - 0.7 * (delta + 0.9 * new_momentum)
    new_local = (0.5 * local_params.astype(jnp.float32) + 0.5 * new_global[None]).astype(jnp.bfloat16)
    blocks = tokens.reshape(N_REP, TOK_REP, D)

    def project(pair):
        rows, weights = pair
        wide = rows.astype(jnp.float32)
        square = lax.optimization_barrier(jnp.mean(wide * wide, axis=1, keepdims=True))
        normed = (wide * lax.rsqrt(square + 1e-05) * norm_gain.astype(jnp.float32)).astype(jnp.bfloat16)
        product = jnp.dot(normed, weights, preferred_element_type=jnp.float32)
        return (product * D ** (-0.5)).astype(jnp.bfloat16)
    keys_values = lax.map(project, (blocks, new_local)).reshape(TOKENS, C)
    return (keys_values, new_local, new_global, new_momentum)
```

```python
import functools

import jax
import jax.numpy as jnp
from jax import lax
from jax.experimental import pallas as pl
from jax.experimental.pallas import tpu as pltpu
from jax.sharding import PartitionSpec as P

MESH = pl.DeviceIdType.MESH
BF16 = jnp.bfloat16
F32 = jnp.float32


def kernel(
    n_rep, n_line, chunk, step,
    counts, gain, tok_hbm, loc_hbm, glob_hbm, mom_hbm,
    kv_out, nl_out, ng_out, nm_out,
    tok, w, loc, glob, mom, got, ag, cnt, acc, kv,
    load_sem, out_sem, cs, cr, rss, rsr, ags, agr, zr, zu, zd, ss, sr,
):
    me = lax.axis_index("rep")
    f = lax.axis_index("fsdp")
    z = f // 2
    core = f % 2
    rows, cols = loc.shape
    part = cols // n_rep
    n_chunk = rows // chunk

    def load(i, src, dst):
        return pltpu.make_async_copy(src, dst, load_sem.at[i])

    loads = [
        load(0, loc_hbm.at[0], loc),
        load(1, glob_hbm, glob),
        load(2, mom_hbm, mom),
        load(3, tok_hbm, tok),
    ]
    for one in loads:
        one.start()
    cnt[me] = jnp.full(cnt.shape[1:], counts[0].astype(F32), F32)

    barrier = pltpu.get_barrier_semaphore()
    for j in range(1, n_rep):
        pl.semaphore_signal(barrier, inc=1, device_id={"rep": (me + j) % n_rep}, device_id_type=MESH)
    pl.semaphore_signal(barrier, inc=1, device_id={"fsdp": z * 2 + 1 - core}, device_id_type=MESH)

    @pl.when(z > 0)
    def _():
        pl.semaphore_signal(barrier, inc=1, device_id={"fsdp": f - 2}, device_id_type=MESH)

    @pl.when(z < n_line - 1)
    def _():
        pl.semaphore_signal(barrier, inc=1, device_id={"fsdp": f + 2}, device_id_type=MESH)

    ends = (z == 0).astype(jnp.int32) + (z == n_line - 1).astype(jnp.int32)
    pl.semaphore_wait(barrier, n_rep + 2 - ends)

    def span(k):
        return pl.ds(pl.multiple_of(k * chunk, chunk), chunk)

    def slot(p):
        return pl.ds(pl.multiple_of(p * part, part), part)

    def count_copy(j, owner):
        return pltpu.make_async_remote_copy(
            cnt.at[owner], cnt.at[owner], cs.at[j - 1], cr.at[j - 1],
            device_id={"rep": (me + j) % n_rep}, device_id_type=MESH)

    def part_copy(j, k):
        to = (me + j) % n_rep
        return pltpu.make_async_remote_copy(
            loc.at[span(k), slot(to)], got.at[me, span(k)], rss.at[j - 1, k], rsr.at[j - 1, k],
            device_id={"rep": to}, device_id_type=MESH)

    def part_wait(j, k):
        owner = (me + n_rep - j) % n_rep
        pltpu.make_async_remote_copy(
            got.at[owner, span(k)], got.at[owner, span(k)], rss.at[j - 1, k], rsr.at[j - 1, k],
            device_id={"rep": (me + j) % n_rep}, device_id_type=MESH).wait_recv()

    def new_copy(j, k, owner):
        return pltpu.make_async_remote_copy(
            ag.at[owner, span(k)], ag.at[owner, span(k)], ags.at[j - 1, k], agr.at[j - 1, k],
            device_id={"rep": (me + j) % n_rep}, device_id_type=MESH)

    def line_copy(src, k, up):
        sem = zu if up else zd
        block = w.at[src * 2 + core, span(k)]
        return pltpu.make_async_remote_copy(
            block, block, sem.at[src, k], zr.at[src, k],
            device_id={"fsdp": f + 2 if up else f - 2}, device_id_type=MESH)

    def pair_copy(src, k, owner):
        block = w.at[src * 2 + owner, span(k)]
        return pltpu.make_async_remote_copy(
            block, block, ss.at[src, k], sr.at[src, k],
            device_id={"fsdp": z * 2 + 1 - core}, device_id_type=MESH)

    def send_parts(k):
        for j in range(1, n_rep):
            part_copy(j, k).start()

    def pass_on(src, k, up, down):
        @pl.when(jnp.logical_and(up, z < n_line - 1))
        def _():
            line_copy(src, k, True).start()

        @pl.when(jnp.logical_and(down, z > 0))
        def _():
            line_copy(src, k, False).start()

        pair_copy(src, k, core).start()

    loads[0].wait()
    for j in range(1, n_rep):
        count_copy(j, me).start()
    ahead = min(2, n_chunk)
    for k in range(ahead):
        send_parts(k)
    loads[1].wait()
    loads[2].wait()
    for j in range(1, n_rep):
        count_copy(j, (me + n_rep - j) % n_rep).wait_recv()
    total = cnt[0, 0:1, :]
    for r in range(1, n_rep):
        total = total + cnt[r, 0:1, :]

    def reduce_chunk(k):
        for j in range(1, n_rep):
            part_wait(j, k)

        def some(i, carry):
            at = pl.ds(pl.multiple_of(k * chunk + i * step, step), step)
            summed = cnt[me, 0:1, :] * loc[at, slot(me)].astype(F32)
            for j in range(1, n_rep):
                r = (me + j) % n_rep
                summed = summed + cnt[r, 0:1, :] * got[r, at, :].astype(F32)
            old = glob[at, :]
            delta = old - summed / total
            moment = 0.9 * mom[at, :] + delta
            new = old - 0.7 * (delta + 0.9 * moment)
            mom[at, :] = moment
            glob[at, :] = new
            ag[me, at, :] = new.astype(BF16)
            return carry

        lax.fori_loop(0, chunk // step, some, 0)
        for j in range(1, n_rep):
            new_copy(j, k, me).start()

    def mix_chunk(k):
        for j in range(1, n_rep):
            new_copy(j, k, (me + n_rep - j) % n_rep).wait_recv()

        def some(i, carry):
            at = pl.ds(pl.multiple_of(k * chunk + i * step, step), step)
            for r in range(n_rep):
                c = slice(r * part, (r + 1) * part)
                mixed = 0.5 * loc[at, c].astype(F32) + 0.5 * ag[r, at, :].astype(F32)
                w[f, at, c] = mixed.astype(BF16)
            return carry

        lax.fori_loop(0, chunk // step, some, 0)
        pass_on(z, k, True, True)

    def norm():
        loads[3].wait()

        def some(i, carry):
            at = pl.ds(pl.multiple_of(i * 16, 16), 16)
            wide = tok[at, :].astype(F32)
            square = jnp.mean(wide * wide, axis=1, keepdims=True)
            tok[at, :] = (wide * lax.rsqrt(square + 1e-05) * gain[...].astype(F32)).astype(BF16)
            return carry

        lax.fori_loop(0, tok.shape[0] // 16, some, 0)
        acc[...] = jnp.zeros_like(acc)

    for k in range(n_chunk):
        reduce_chunk(k)
        if k + ahead < n_chunk:
            send_parts(k + ahead)
        if k >= 1:
            mix_chunk(k - 1)
        if k == min(1, n_chunk - 1):
            norm()
    mix_chunk(n_chunk - 1)

    outs = [
        pltpu.make_async_copy(glob, ng_out, out_sem.at[0]),
        pltpu.make_async_copy(mom, nm_out, out_sem.at[1]),
        pltpu.make_async_copy(w.at[f], nl_out.at[0], out_sem.at[2]),
    ]
    for one in outs:
        one.start()

    wide_cols = min(256, cols)

    def multiply(at, k):
        a = tok[:, pl.ds(pl.multiple_of(at * rows + k * chunk, chunk), chunk)]

        def some(i, carry):
            c = pl.ds(pl.multiple_of(i * wide_cols, wide_cols), wide_cols)
            acc[:, c] += jnp.dot(a, w[at, span(k), c], preferred_element_type=F32)
            return carry

        lax.fori_loop(0, cols // wide_cols, some, 0)

    def compute(src, k):
        multiply(src * 2 + core, k)
        pair_copy(src, k, 1 - core).wait_recv()
        multiply(src * 2 + 1 - core, k)

    def own(k, carry):
        compute(z, k)
        return carry

    def receive(t):
        d = t // n_chunk
        k = t % n_chunk

        @pl.when(z - d >= 0)
        def _():
            line_copy(z - d, k, True).wait_recv()
            pass_on(z - d, k, True, False)

        @pl.when(z + d < n_line)
        def _():
            line_copy(z + d, k, False).wait_recv()
            pass_on(z + d, k, False, True)

    def finish(t):
        d = t // n_chunk
        k = t % n_chunk

        @pl.when(z - d >= 0)
        def _():
            compute(z - d, k)

        @pl.when(jnp.logical_and(z + d < n_line, d > 0))
        def _():
            compute(z + d, k)

    def event(t, carry):
        receive(t)
        finish(t - n_chunk)
        return carry

    n_event = n_line * n_chunk
    lag = 1
    for t in range(min(lag, n_event - n_chunk)):
        receive(n_chunk + t)
    lax.fori_loop(0, n_chunk, own, 0)

    def later(t, carry):
        receive(t)
        finish(t - lag)
        return carry

    lax.fori_loop(n_chunk + lag, n_event, later, 0)
    for t in range(n_event - lag, n_event):
        finish(t)

    scale = (n_line * 2 * rows) ** (-0.5)

    def scaled(i, carry):
        at = pl.ds(pl.multiple_of(i * 64, 64), 64)
        kv[at, :] = (acc[at, :] * scale).astype(BF16)
        return carry

    lax.fori_loop(0, acc.shape[0] // 64, scaled, 0)
    last = pltpu.make_async_copy(kv, kv_out, out_sem.at[3])
    last.start()

    for j in range(1, n_rep):
        count_copy(j, me).wait_send()

    def sent(k, carry):
        for j in range(1, n_rep):
            part_copy(j, k).wait_send()
            new_copy(j, k, me).wait_send()
        return carry

    lax.fori_loop(0, n_chunk, sent, 0)

    def passed(t, carry):
        src = t // n_chunk
        k = t % n_chunk

        @pl.when(jnp.logical_and(src <= z, z < n_line - 1))
        def _():
            line_copy(src, k, True).wait_send()

        @pl.when(jnp.logical_and(src >= z, z > 0))
        def _():
            line_copy(src, k, False).wait_send()

        pair_copy(src, k, core).wait_send()
        return carry

    lax.fori_loop(0, n_event, passed, 0)
    for one in outs:
        one.wait()
    last.wait()


def shards(n_rep, n_fsdp, tokens, norm_gain, step_counts, local_params, global_params, momentum):
    count, width = tokens.shape
    _, rows, cols = local_params.shape
    part = cols // n_rep
    n_line = n_fsdp // 2
    chunk = min(128, rows)
    n_chunk = rows // chunk
    anywhere = pl.BlockSpec(memory_space=pl.ANY)
    dma = pltpu.SemaphoreType.DMA
    return pl.pallas_call(
        functools.partial(kernel, n_rep, n_line, chunk, 32),
        out_shape=(
            jax.ShapeDtypeStruct((count, cols), BF16),
            jax.ShapeDtypeStruct((1, rows, cols), BF16),
            jax.ShapeDtypeStruct((rows, part), F32),
            jax.ShapeDtypeStruct((rows, part), F32),
        ),
        in_specs=[
            pl.BlockSpec(memory_space=pltpu.SMEM),
            pl.BlockSpec(memory_space=pltpu.VMEM),
            anywhere, anywhere, anywhere, anywhere,
        ],
        out_specs=(anywhere,) * 4,
        scratch_shapes=[
            pltpu.VMEM((count, width), BF16),
            pltpu.VMEM((n_fsdp, rows, cols), BF16),
            pltpu.VMEM((rows, cols), BF16),
            pltpu.VMEM((rows, part), F32),
            pltpu.VMEM((rows, part), F32),
            pltpu.VMEM((n_rep, rows, part), BF16),
            pltpu.VMEM((n_rep, rows, part), BF16),
            pltpu.VMEM((n_rep, 8, part), F32),
            pltpu.VMEM((count, cols), F32),
            pltpu.VMEM((count, cols), BF16),
            dma((4,)), dma((4,)),
            dma((n_rep - 1,)), dma((n_rep - 1,)),
            dma((n_rep - 1, n_chunk)), dma((n_rep - 1, n_chunk)),
            dma((n_rep - 1, n_chunk)), dma((n_rep - 1, n_chunk)),
            dma((n_line, n_chunk)), dma((n_line, n_chunk)), dma((n_line, n_chunk)),
            dma((n_line, n_chunk)), dma((n_line, n_chunk)),
        ],
        compiler_params=pltpu.CompilerParams(
            collective_id=0, has_side_effects=True, vmem_limit_bytes=56 * 2**20
        ),
    )(step_counts, norm_gain.reshape(1, width), tokens, local_params, global_params, momentum)


def solution(mesh):
    return jax.shard_map(
        functools.partial(shards, mesh.shape["rep"], mesh.shape["fsdp"]),
        mesh=mesh,
        in_specs=(
            P(("rep", "fsdp"), None),
            P(),
            P("rep"),
            P("rep", "fsdp", None),
            P("fsdp", "rep"),
            P("fsdp", "rep"),
        ),
        out_specs=(
            P(("rep", "fsdp"), None),
            P("rep", "fsdp", None),
            P("fsdp", "rep"),
            P("fsdp", "rep"),
        ),
        check_vma=False,
    )
```

```python
import functools

import jax
import jax.numpy as jnp
from jax import lax
from jax.experimental import pallas as pl
from jax.experimental.pallas import tpu as pltpu
from jax.sharding import PartitionSpec as P

MESH = pl.DeviceIdType.MESH
BF16 = jnp.bfloat16
F32 = jnp.float32


def kernel(
    n_rep, n_line, chunk, step, first,
    counts, gain, tok_hbm, loc_hbm, glob_hbm, mom_hbm,
    kv_out, nl_out, ng_out, nm_out,
    tok, w, loc, glob, mom, got, ag, cnt, acc, kv, lent, part_out, part_in,
    load_sem, out_sem, cs, cr, rss, rsr, ags, agr, zr, zu, zd, ss, sr, ts, tr, ps, pr,
):
    me = lax.axis_index("rep")
    f = lax.axis_index("fsdp")
    z = f // 2
    core = f % 2
    rows, cols = loc.shape
    part = cols // n_rep
    n_chunk = rows // chunk
    at_end = jnp.logical_or(z == 0, z == n_line - 1)
    helps = jnp.logical_or(z == 1, z == n_line - 2)
    low = z < n_line // 2
    inward = jnp.where(low, f + 2, f - 2)
    outward = jnp.where(low, f - 2, f + 2)
    lend = first < n_chunk

    def lent_out(dest, src, k):
        if not lend:
            return dest < 0
        dist = jnp.where(dest == 0, src, n_line - 1 - src)
        near = jnp.logical_or(dist == 1, dist == 2)
        end = jnp.logical_or(dest == 0, dest == n_line - 1)
        return jnp.logical_and(jnp.logical_and(end, near), k >= first)

    def goes_up(src, k):
        return jnp.logical_and(z < n_line - 1, jnp.logical_not(lent_out(z + 1, src, k)))

    def goes_down(src, k):
        return jnp.logical_and(z > 0, jnp.logical_not(lent_out(z - 1, src, k)))

    def load(i, src, dst):
        return pltpu.make_async_copy(src, dst, load_sem.at[i])

    loads = [
        load(0, loc_hbm.at[0], loc),
        load(1, glob_hbm, glob),
        load(2, mom_hbm, mom),
        load(3, tok_hbm, tok),
    ]
    for one in loads:
        one.start()
    cnt[me] = jnp.full(cnt.shape[1:], counts[0].astype(F32), F32)

    barrier = pltpu.get_barrier_semaphore()
    for j in range(1, n_rep):
        pl.semaphore_signal(barrier, inc=1, device_id={"rep": (me + j) % n_rep}, device_id_type=MESH)
    pl.semaphore_signal(barrier, inc=1, device_id={"fsdp": z * 2 + 1 - core}, device_id_type=MESH)

    @pl.when(z > 0)
    def _():
        pl.semaphore_signal(barrier, inc=1, device_id={"fsdp": f - 2}, device_id_type=MESH)

    @pl.when(z < n_line - 1)
    def _():
        pl.semaphore_signal(barrier, inc=1, device_id={"fsdp": f + 2}, device_id_type=MESH)

    ends = (z == 0).astype(jnp.int32) + (z == n_line - 1).astype(jnp.int32)
    pl.semaphore_wait(barrier, n_rep + 2 - ends)

    def span(k):
        return pl.ds(pl.multiple_of(k * chunk, chunk), chunk)

    def slot(p):
        return pl.ds(pl.multiple_of(p * part, part), part)

    def count_copy(j, owner):
        return pltpu.make_async_remote_copy(
            cnt.at[owner], cnt.at[owner], cs.at[j - 1], cr.at[j - 1],
            device_id={"rep": (me + j) % n_rep}, device_id_type=MESH)

    def part_copy(j, k):
        to = (me + j) % n_rep
        return pltpu.make_async_remote_copy(
            loc.at[span(k), slot(to)], got.at[me, span(k)], rss.at[j - 1, k], rsr.at[j - 1, k],
            device_id={"rep": to}, device_id_type=MESH)

    def part_wait(j, k):
        owner = (me + n_rep - j) % n_rep
        pltpu.make_async_remote_copy(
            got.at[owner, span(k)], got.at[owner, span(k)], rss.at[j - 1, k], rsr.at[j - 1, k],
            device_id={"rep": (me + j) % n_rep}, device_id_type=MESH).wait_recv()

    def new_copy(j, k, owner):
        return pltpu.make_async_remote_copy(
            ag.at[owner, span(k)], ag.at[owner, span(k)], ags.at[j - 1, k], agr.at[j - 1, k],
            device_id={"rep": (me + j) % n_rep}, device_id_type=MESH)

    def line_copy(src, k, up):
        sem = zu if up else zd
        block = w.at[src * 2 + core, span(k)]
        return pltpu.make_async_remote_copy(
            block, block, sem.at[src, k], zr.at[src, k],
            device_id={"fsdp": f + 2 if up else f - 2}, device_id_type=MESH)

    def pair_copy(src, k, owner):
        block = w.at[src * 2 + owner, span(k)]
        return pltpu.make_async_remote_copy(
            block, block, ss.at[src, k], sr.at[src, k],
            device_id={"fsdp": z * 2 + 1 - core}, device_id_type=MESH)

    def send_parts(k):
        for j in range(1, n_rep):
            part_copy(j, k).start()

    def pass_on(src, k, up, down):
        @pl.when(jnp.logical_and(up, goes_up(src, k)))
        def _():
            line_copy(src, k, True).start()

        @pl.when(jnp.logical_and(down, goes_down(src, k)))
        def _():
            line_copy(src, k, False).start()

        pair_copy(src, k, core).start()

    def lent_block(q, low_end):
        d = q // 2 + 1
        return jnp.where(low_end, d, n_line - 1 - d) * 2 + q % 2

    lent_rows = rows - first * chunk

    def lent_copy(q):
        at = pl.multiple_of(lent_block(q, low) * rows + first * chunk, chunk)
        return pltpu.make_async_remote_copy(
            tok.at[:, pl.ds(at, lent_rows)], lent.at[q], ts.at[q], tr.at[q],
            device_id={"fsdp": inward}, device_id_type=MESH)

    wide_cols = min(256, cols)
    n_wide = cols // wide_cols

    def part_back(i):
        c = slice(i * wide_cols, (i + 1) * wide_cols)
        return pltpu.make_async_remote_copy(
            part_out.at[:, c], part_in.at[:, c], ps.at[i], pr.at[i],
            device_id={"fsdp": outward}, device_id_type=MESH)

    def help_end():
        for q in range(4):
            lent_copy(q).wait_recv()
        for i in range(n_wide):
            c = slice(i * wide_cols, (i + 1) * wide_cols)
            summed = jnp.zeros((tok.shape[0], wide_cols), F32)
            for q in range(4):
                summed = summed + jnp.dot(
                    lent[q], w[lent_block(q, low), first * chunk :, c], preferred_element_type=F32)
            part_out[:, c] = summed.astype(BF16)
            part_back(i).start()

    loads[0].wait()
    for j in range(1, n_rep):
        count_copy(j, me).start()
    ahead = min(2, n_chunk)
    for k in range(ahead):
        send_parts(k)
    loads[1].wait()
    loads[2].wait()
    for j in range(1, n_rep):
        count_copy(j, (me + n_rep - j) % n_rep).wait_recv()
    total = cnt[0, 0:1, :]
    for r in range(1, n_rep):
        total = total + cnt[r, 0:1, :]

    def reduce_chunk(k):
        for j in range(1, n_rep):
            part_wait(j, k)

        def some(i, carry):
            at = pl.ds(pl.multiple_of(k * chunk + i * step, step), step)
            summed = cnt[me, 0:1, :] * loc[at, slot(me)].astype(F32)
            for j in range(1, n_rep):
                r = (me + j) % n_rep
                summed = summed + cnt[r, 0:1, :] * got[r, at, :].astype(F32)
            old = glob[at, :]
            delta = old - summed / total
            moment = 0.9 * mom[at, :] + delta
            new = old - 0.7 * (delta + 0.9 * moment)
            mom[at, :] = moment
            glob[at, :] = new
            ag[me, at, :] = new.astype(BF16)
            return carry

        lax.fori_loop(0, chunk // step, some, 0)
        for j in range(1, n_rep):
            new_copy(j, k, me).start()

    def mix_chunk(k):
        for j in range(1, n_rep):
            new_copy(j, k, (me + n_rep - j) % n_rep).wait_recv()

        def some(i, carry):
            at = pl.ds(pl.multiple_of(k * chunk + i * step, step), step)
            for r in range(n_rep):
                c = slice(r * part, (r + 1) * part)
                mixed = 0.5 * loc[at, c].astype(F32) + 0.5 * ag[r, at, :].astype(F32)
                w[f, at, c] = mixed.astype(BF16)
            return carry

        lax.fori_loop(0, chunk // step, some, 0)
        inner = jnp.logical_not(at_end) if lend else True
        pass_on(z, k, inner, inner)

    def norm():
        loads[3].wait()

        def some(i, carry):
            at = pl.ds(pl.multiple_of(i * 16, 16), 16)
            wide = tok[at, :].astype(F32)
            square = jnp.mean(wide * wide, axis=1, keepdims=True)
            tok[at, :] = (wide * lax.rsqrt(square + 1e-05) * gain[...].astype(F32)).astype(BF16)
            return carry

        lax.fori_loop(0, tok.shape[0] // 16, some, 0)
        acc[...] = jnp.zeros_like(acc)

    if lend:
        @pl.when(at_end)
        def _():
            norm()
            for q in range(4):
                lent_copy(q).start()

    for k in range(n_chunk):
        reduce_chunk(k)
        if k + ahead < n_chunk:
            send_parts(k + ahead)
        if k >= 1:
            mix_chunk(k - 1)
    mix_chunk(n_chunk - 1)

    if lend:
        @pl.when(at_end)
        def _():
            for q in range(4):
                lent_copy(q).wait_send()

        @pl.when(z == 0)
        def _():
            for k in range(n_chunk):
                line_copy(z, k, True).start()

        @pl.when(z == n_line - 1)
        def _():
            for k in range(n_chunk):
                line_copy(z, k, False).start()

        @pl.when(jnp.logical_not(at_end))
        def _():
            norm()
    else:
        norm()

    outs = [
        pltpu.make_async_copy(glob, ng_out, out_sem.at[0]),
        pltpu.make_async_copy(mom, nm_out, out_sem.at[1]),
        pltpu.make_async_copy(w.at[f], nl_out.at[0], out_sem.at[2]),
    ]
    for one in outs:
        one.start()

    def multiply(at, k):
        a = tok[:, pl.ds(pl.multiple_of(at * rows + k * chunk, chunk), chunk)]

        def some(i, carry):
            c = pl.ds(pl.multiple_of(i * wide_cols, wide_cols), wide_cols)
            acc[:, c] += jnp.dot(a, w[at, span(k), c], preferred_element_type=F32)
            return carry

        lax.fori_loop(0, cols // wide_cols, some, 0)

    def compute(src, k):
        multiply(src * 2 + core, k)
        pair_copy(src, k, 1 - core).wait_recv()
        multiply(src * 2 + 1 - core, k)

    def own(k, carry):
        compute(z, k)
        return carry

    base = n_chunk * jnp.maximum(jnp.maximum(z - 1, n_line - 2 - z), 0)

    def arrival(t, up):
        room = z if up else n_line - 1 - z
        early = t < base
        k = jnp.where(early, t % n_chunk, t - base - room)
        dist = jnp.where(early, t // n_chunk + 1, room)
        src = z - dist if up else z + dist
        inside = jnp.where(early, dist < room, room > 0)
        there = jnp.logical_and(inside, jnp.logical_and(k >= 0, k < n_chunk))
        return jnp.logical_and(there, jnp.logical_not(lent_out(z, src, k))), src, k

    def receive(t):
        for up in (True, False):
            there, src, k = arrival(t, up)

            @pl.when(there)
            def _():
                line_copy(src, k, up).wait_recv()
                pass_on(src, k, up, not up)

    def finish(t):
        for up in (True, False):
            there, src, k = arrival(t, up)

            @pl.when(there)
            def _():
                compute(src, k)

    n_event = n_line * n_chunk
    n_tick = (n_line - 2) * n_chunk + n_chunk + n_line
    receive(0)
    lax.fori_loop(0, n_chunk, own, 0)

    def later(t, carry):
        receive(t)
        finish(t - 1)
        if lend:
            @pl.when(jnp.logical_and(helps, t == base))
            def _():
                help_end()
        return carry

    lax.fori_loop(1, n_tick + 1, later, 0)

    scale = (n_line * 2 * rows) ** (-0.5)

    def scaled(i, carry):
        at = pl.ds(pl.multiple_of(i * 64, 64), 64)
        kv[at, :] = (acc[at, :] * scale).astype(BF16)
        return carry

    if lend:
        @pl.when(at_end)
        def _():
            for i in range(n_wide):
                part_back(i).wait_recv()

            def add(i, carry):
                at = pl.ds(pl.multiple_of(i * 64, 64), 64)
                acc[at, :] += part_in[at, :].astype(F32)
                return carry

            lax.fori_loop(0, acc.shape[0] // 64, add, 0)

        @pl.when(helps)
        def _():
            for i in range(n_wide):
                part_back(i).wait_send()

    lax.fori_loop(0, acc.shape[0] // 64, scaled, 0)
    last = pltpu.make_async_copy(kv, kv_out, out_sem.at[3])
    last.start()

    for j in range(1, n_rep):
        count_copy(j, me).wait_send()

    def sent(k, carry):
        for j in range(1, n_rep):
            part_copy(j, k).wait_send()
            new_copy(j, k, me).wait_send()
        return carry

    lax.fori_loop(0, n_chunk, sent, 0)

    def passed(t, carry):
        src = t // n_chunk
        k = t % n_chunk

        @pl.when(jnp.logical_and(src <= z, goes_up(src, k)))
        def _():
            line_copy(src, k, True).wait_send()

        @pl.when(jnp.logical_and(src >= z, goes_down(src, k)))
        def _():
            line_copy(src, k, False).wait_send()

        @pl.when(jnp.logical_not(lent_out(z, src, k)))
        def _():
            pair_copy(src, k, core).wait_send()
        return carry

    lax.fori_loop(0, n_event, passed, 0)
    for one in outs:
        one.wait()
    last.wait()


def shards(n_rep, n_fsdp, tokens, norm_gain, step_counts, local_params, global_params, momentum):
    count, width = tokens.shape
    _, rows, cols = local_params.shape
    part = cols // n_rep
    n_line = n_fsdp // 2
    chunk = min(128, rows)
    n_chunk = rows // chunk
    first = n_chunk // 2 if n_line >= 4 else n_chunk
    lent_rows = max(rows - first * chunk, 128)
    anywhere = pl.BlockSpec(memory_space=pl.ANY)
    dma = pltpu.SemaphoreType.DMA
    return pl.pallas_call(
        functools.partial(kernel, n_rep, n_line, chunk, 32, first),
        out_shape=(
            jax.ShapeDtypeStruct((count, cols), BF16),
            jax.ShapeDtypeStruct((1, rows, cols), BF16),
            jax.ShapeDtypeStruct((rows, part), F32),
            jax.ShapeDtypeStruct((rows, part), F32),
        ),
        in_specs=[
            pl.BlockSpec(memory_space=pltpu.SMEM),
            pl.BlockSpec(memory_space=pltpu.VMEM),
            anywhere, anywhere, anywhere, anywhere,
        ],
        out_specs=(anywhere,) * 4,
        scratch_shapes=[
            pltpu.VMEM((count, width), BF16),
            pltpu.VMEM((n_fsdp, rows, cols), BF16),
            pltpu.VMEM((rows, cols), BF16),
            pltpu.VMEM((rows, part), F32),
            pltpu.VMEM((rows, part), F32),
            pltpu.VMEM((n_rep, rows, part), BF16),
            pltpu.VMEM((n_rep, rows, part), BF16),
            pltpu.VMEM((n_rep, 8, part), F32),
            pltpu.VMEM((count, cols), F32),
            pltpu.VMEM((count, cols), BF16),
            pltpu.VMEM((4, count, lent_rows), BF16),
            pltpu.VMEM((count, cols), BF16),
            pltpu.VMEM((count, cols), BF16),
            dma((4,)), dma((4,)),
            dma((n_rep - 1,)), dma((n_rep - 1,)),
            dma((n_rep - 1, n_chunk)), dma((n_rep - 1, n_chunk)),
            dma((n_rep - 1, n_chunk)), dma((n_rep - 1, n_chunk)),
            dma((n_line, n_chunk)), dma((n_line, n_chunk)), dma((n_line, n_chunk)),
            dma((n_line, n_chunk)), dma((n_line, n_chunk)),
            dma((4,)), dma((4,)), dma((max(cols // 256, 1),)), dma((max(cols // 256, 1),)),
        ],
        compiler_params=pltpu.CompilerParams(
            collective_id=0, has_side_effects=True, vmem_limit_bytes=60 * 2**20
        ),
    )(step_counts, norm_gain.reshape(1, width), tokens, local_params, global_params, momentum)


def solution(mesh):
    return jax.shard_map(
        functools.partial(shards, mesh.shape["rep"], mesh.shape["fsdp"]),
        mesh=mesh,
        in_specs=(
            P(("rep", "fsdp"), None),
            P(),
            P("rep"),
            P("rep", "fsdp", None),
            P("fsdp", "rep"),
            P("fsdp", "rep"),
        ),
        out_specs=(
            P(("rep", "fsdp"), None),
            P("rep", "fsdp", None),
            P("fsdp", "rep"),
            P("fsdp", "rep"),
        ),
        check_vma=False,
    )
```

```python
import functools

import jax
import jax.numpy as jnp
from jax import lax
from jax.experimental import pallas as pl
from jax.experimental.pallas import tpu as pltpu
from jax.sharding import PartitionSpec as P

MESH = pl.DeviceIdType.MESH
BF16 = jnp.bfloat16
F32 = jnp.float32


def kernel(
    n_rep, n_line, chunk, step, first,
    counts, gain, tok_hbm, loc_hbm, glob_hbm, mom_hbm,
    kv_out, nl_out, ng_out, nm_out,
    tok, w, loc, glob, mom, got, ag, cnt, acc, kv, lent, part_out, part_in,
    load_sem, out_sem, cs, cr, rss, rsr, ags, agr, zr, zu, zd, ss, sr, ts, tr, ps, pr,
):
    me = lax.axis_index("rep")
    f = lax.axis_index("fsdp")
    z = f // 2
    core = f % 2
    rows, cols = loc.shape
    part = cols // n_rep
    n_chunk = rows // chunk
    at_end = jnp.logical_or(z == 0, z == n_line - 1)
    helps = jnp.logical_or(z == 1, z == n_line - 2)
    low = z < n_line // 2
    inward = jnp.where(low, f + 2, f - 2)
    outward = jnp.where(low, f - 2, f + 2)
    lend = first < n_chunk

    def lent_out(dest, src, k):
        if not lend:
            return dest < 0
        dist = jnp.where(dest == 0, src, n_line - 1 - src)
        near = jnp.logical_or(dist == 1, dist == 2)
        end = jnp.logical_or(dest == 0, dest == n_line - 1)
        return jnp.logical_and(jnp.logical_and(end, near), k >= first)

    def goes_up(src, k):
        return jnp.logical_and(z < n_line - 1, jnp.logical_not(lent_out(z + 1, src, k)))

    def goes_down(src, k):
        return jnp.logical_and(z > 0, jnp.logical_not(lent_out(z - 1, src, k)))

    def load(i, src, dst):
        return pltpu.make_async_copy(src, dst, load_sem.at[i])

    loads = [
        load(0, loc_hbm.at[0], loc),
        load(1, glob_hbm, glob),
        load(2, mom_hbm, mom),
        load(3, tok_hbm, tok),
    ]
    for one in loads:
        one.start()
    cnt[me] = jnp.full(cnt.shape[1:], counts[0].astype(F32), F32)

    barrier = pltpu.get_barrier_semaphore()
    for j in range(1, n_rep):
        pl.semaphore_signal(barrier, inc=1, device_id={"rep": (me + j) % n_rep}, device_id_type=MESH)
    pl.semaphore_signal(barrier, inc=1, device_id={"fsdp": z * 2 + 1 - core}, device_id_type=MESH)

    @pl.when(z > 0)
    def _():
        pl.semaphore_signal(barrier, inc=1, device_id={"fsdp": f - 2}, device_id_type=MESH)

    @pl.when(z < n_line - 1)
    def _():
        pl.semaphore_signal(barrier, inc=1, device_id={"fsdp": f + 2}, device_id_type=MESH)

    ends = (z == 0).astype(jnp.int32) + (z == n_line - 1).astype(jnp.int32)
    pl.semaphore_wait(barrier, n_rep + 2 - ends)

    def span(k):
        return pl.ds(pl.multiple_of(k * chunk, chunk), chunk)

    def slot(p):
        return pl.ds(pl.multiple_of(p * part, part), part)

    def count_copy(j, owner):
        return pltpu.make_async_remote_copy(
            cnt.at[owner], cnt.at[owner], cs.at[j - 1], cr.at[j - 1],
            device_id={"rep": (me + j) % n_rep}, device_id_type=MESH)

    def part_copy(j, k):
        to = (me + j) % n_rep
        return pltpu.make_async_remote_copy(
            loc.at[span(k), slot(to)], got.at[me, span(k)], rss.at[j - 1, k], rsr.at[j - 1, k],
            device_id={"rep": to}, device_id_type=MESH)

    def part_wait(j, k):
        owner = (me + n_rep - j) % n_rep
        pltpu.make_async_remote_copy(
            got.at[owner, span(k)], got.at[owner, span(k)], rss.at[j - 1, k], rsr.at[j - 1, k],
            device_id={"rep": (me + j) % n_rep}, device_id_type=MESH).wait_recv()

    def new_copy(j, k, owner):
        return pltpu.make_async_remote_copy(
            ag.at[owner, span(k)], ag.at[owner, span(k)], ags.at[j - 1, k], agr.at[j - 1, k],
            device_id={"rep": (me + j) % n_rep}, device_id_type=MESH)

    def line_copy(src, k, up):
        sem = zu if up else zd
        block = w.at[src * 2 + core, span(k)]
        return pltpu.make_async_remote_copy(
            block, block, sem.at[src, k], zr.at[src, k],
            device_id={"fsdp": f + 2 if up else f - 2}, device_id_type=MESH)

    def pair_copy(src, k, owner):
        block = w.at[src * 2 + owner, span(k)]
        return pltpu.make_async_remote_copy(
            block, block, ss.at[src, k], sr.at[src, k],
            device_id={"fsdp": z * 2 + 1 - core}, device_id_type=MESH)

    def send_parts(k):
        for j in range(1, n_rep):
            part_copy(j, k).start()

    def pass_on(src, k, up, down):
        @pl.when(jnp.logical_and(up, goes_up(src, k)))
        def _():
            line_copy(src, k, True).start()

        @pl.when(jnp.logical_and(down, goes_down(src, k)))
        def _():
            line_copy(src, k, False).start()

        pair_copy(src, k, core).start()

    def lent_block(q, low_end):
        d = q // 2 + 1
        return jnp.where(low_end, d, n_line - 1 - d) * 2 + q % 2

    lent_rows = rows - first * chunk

    def lent_copy(q):
        at = pl.multiple_of(lent_block(q, low) * rows + first * chunk, chunk)
        return pltpu.make_async_remote_copy(
            tok.at[:, pl.ds(at, lent_rows)], lent.at[q], ts.at[q], tr.at[q],
            device_id={"fsdp": inward}, device_id_type=MESH)

    wide_cols = min(256, cols)
    n_wide = cols // wide_cols

    def part_back(i):
        c = slice(i * wide_cols, (i + 1) * wide_cols)
        return pltpu.make_async_remote_copy(
            part_out.at[:, c], part_in.at[:, c], ps.at[i], pr.at[i],
            device_id={"fsdp": outward}, device_id_type=MESH)

    def help_end():
        for q in range(4):
            lent_copy(q).wait_recv()
        for i in range(n_wide):
            c = slice(i * wide_cols, (i + 1) * wide_cols)
            summed = jnp.zeros((tok.shape[0], wide_cols), F32)
            for q in range(4):
                summed = summed + jnp.dot(
                    lent[q], w[lent_block(q, low), first * chunk :, c], preferred_element_type=F32)
            part_out[:, c] = summed.astype(BF16)
            part_back(i).start()

    loads[0].wait()
    for j in range(1, n_rep):
        count_copy(j, me).start()
    ahead = min(2, n_chunk)
    for k in range(ahead):
        send_parts(k)
    loads[1].wait()
    loads[2].wait()
    for j in range(1, n_rep):
        count_copy(j, (me + n_rep - j) % n_rep).wait_recv()
    total = cnt[0, 0:1, :]
    for r in range(1, n_rep):
        total = total + cnt[r, 0:1, :]

    def reduce_chunk(k):
        for j in range(1, n_rep):
            part_wait(j, k)

        def some(i, carry):
            at = pl.ds(pl.multiple_of(k * chunk + i * step, step), step)
            summed = cnt[me, 0:1, :] * loc[at, slot(me)].astype(F32)
            for j in range(1, n_rep):
                r = (me + j) % n_rep
                summed = summed + cnt[r, 0:1, :] * got[r, at, :].astype(F32)
            old = glob[at, :]
            delta = old - summed / total
            moment = 0.9 * mom[at, :] + delta
            new = old - 0.7 * (delta + 0.9 * moment)
            mom[at, :] = moment
            glob[at, :] = new
            ag[me, at, :] = new.astype(BF16)
            return carry

        lax.fori_loop(0, chunk // step, some, 0)
        for j in range(1, n_rep):
            new_copy(j, k, me).start()

    def mix_chunk(k):
        for j in range(1, n_rep):
            new_copy(j, k, (me + n_rep - j) % n_rep).wait_recv()

        def some(i, carry):
            at = pl.ds(pl.multiple_of(k * chunk + i * step, step), step)
            for r in range(n_rep):
                c = slice(r * part, (r + 1) * part)
                mixed = 0.5 * loc[at, c].astype(F32) + 0.5 * ag[r, at, :].astype(F32)
                w[f, at, c] = mixed.astype(BF16)
            return carry

        lax.fori_loop(0, chunk // step, some, 0)
        inner = jnp.logical_not(at_end) if lend else True
        pass_on(z, k, inner, inner)

    def norm():
        loads[3].wait()

        def some(i, carry):
            at = pl.ds(pl.multiple_of(i * 16, 16), 16)
            wide = tok[at, :].astype(F32)
            square = jnp.mean(wide * wide, axis=1, keepdims=True)
            tok[at, :] = (wide * lax.rsqrt(square + 1e-05) * gain[...].astype(F32)).astype(BF16)
            return carry

        lax.fori_loop(0, tok.shape[0] // 16, some, 0)
        acc[...] = jnp.zeros_like(acc)

    if lend:
        @pl.when(at_end)
        def _():
            norm()
            for q in range(4):
                lent_copy(q).start()

    def multiply(at, k):
        a = tok[:, pl.ds(pl.multiple_of(at * rows + k * chunk, chunk), chunk)]

        def some(i, carry):
            c = pl.ds(pl.multiple_of(i * wide_cols, wide_cols), wide_cols)
            acc[:, c] += jnp.dot(a, w[at, span(k), c], preferred_element_type=F32)
            return carry

        lax.fori_loop(0, cols // wide_cols, some, 0)

    def compute(src, k):
        multiply(src * 2 + core, k)
        pair_copy(src, k, 1 - core).wait_recv()
        multiply(src * 2 + 1 - core, k)

    def own(k, carry):
        compute(z, k)
        return carry

    base = n_chunk * jnp.maximum(jnp.maximum(z - 1, n_line - 2 - z), 0)

    def arrival(t, up):
        room = z if up else n_line - 1 - z
        early = t < base
        k = jnp.where(early, t % n_chunk, t - base - room)
        dist = jnp.where(early, t // n_chunk + 1, room)
        src = z - dist if up else z + dist
        inside = jnp.where(early, dist < room, room > 0)
        there = jnp.logical_and(inside, jnp.logical_and(k >= 0, k < n_chunk))
        return jnp.logical_and(there, jnp.logical_not(lent_out(z, src, k))), src, k

    def receive(t):
        for up in (True, False):
            there, src, k = arrival(t, up)

            @pl.when(there)
            def _():
                line_copy(src, k, up).wait_recv()
                pass_on(src, k, up, not up)

    def finish(t):
        for up in (True, False):
            there, src, k = arrival(t, up)

            @pl.when(there)
            def _():
                compute(src, k)

    n_event = n_line * n_chunk
    n_tick = (n_line - 2) * n_chunk + n_chunk + n_line
    hold = 1
    for k in range(n_chunk + 1):
        if k < n_chunk:
            reduce_chunk(k)
            if k + ahead < n_chunk:
                send_parts(k + ahead)
        if k == 0:
            if lend:
                pl.when(jnp.logical_not(at_end))(norm)
            else:
                norm()
        if k >= 1:
            mix_chunk(k - 1)
        if k >= 1 + hold:
            t = k - 1 - hold
            receive(t)
            own(t, 0)
            if t >= 1:
                finish(t - 1)
    caught = n_chunk - hold

    if lend:
        @pl.when(at_end)
        def _():
            for q in range(4):
                lent_copy(q).wait_send()

        @pl.when(z == 0)
        def _():
            for k in range(n_chunk):
                line_copy(z, k, True).start()

        @pl.when(z == n_line - 1)
        def _():
            for k in range(n_chunk):
                line_copy(z, k, False).start()

    outs = [
        pltpu.make_async_copy(glob, ng_out, out_sem.at[0]),
        pltpu.make_async_copy(mom, nm_out, out_sem.at[1]),
        pltpu.make_async_copy(w.at[f], nl_out.at[0], out_sem.at[2]),
    ]
    for one in outs:
        one.start()

    receive(caught)
    if caught >= 1:
        finish(caught - 1)
    for k in range(caught, n_chunk):
        own(k, 0)

    def later(t, carry):
        receive(t)
        finish(t - 1)
        if lend:
            @pl.when(jnp.logical_and(helps, t == base))
            def _():
                help_end()
        return carry

    lax.fori_loop(caught + 1, n_tick + 1, later, 0)

    scale = (n_line * 2 * rows) ** (-0.5)

    def scaled(i, carry):
        at = pl.ds(pl.multiple_of(i * 64, 64), 64)
        kv[at, :] = (acc[at, :] * scale).astype(BF16)
        return carry

    if lend:
        @pl.when(at_end)
        def _():
            for i in range(n_wide):
                part_back(i).wait_recv()

            def add(i, carry):
                at = pl.ds(pl.multiple_of(i * 64, 64), 64)
                acc[at, :] += part_in[at, :].astype(F32)
                return carry

            lax.fori_loop(0, acc.shape[0] // 64, add, 0)

        @pl.when(helps)
        def _():
            for i in range(n_wide):
                part_back(i).wait_send()

    lax.fori_loop(0, acc.shape[0] // 64, scaled, 0)
    last = pltpu.make_async_copy(kv, kv_out, out_sem.at[3])
    last.start()

    for j in range(1, n_rep):
        count_copy(j, me).wait_send()

    def sent(k, carry):
        for j in range(1, n_rep):
            part_copy(j, k).wait_send()
            new_copy(j, k, me).wait_send()
        return carry

    lax.fori_loop(0, n_chunk, sent, 0)

    def passed(t, carry):
        src = t // n_chunk
        k = t % n_chunk

        @pl.when(jnp.logical_and(src <= z, goes_up(src, k)))
        def _():
            line_copy(src, k, True).wait_send()

        @pl.when(jnp.logical_and(src >= z, goes_down(src, k)))
        def _():
            line_copy(src, k, False).wait_send()

        @pl.when(jnp.logical_not(lent_out(z, src, k)))
        def _():
            pair_copy(src, k, core).wait_send()
        return carry

    lax.fori_loop(0, n_event, passed, 0)
    for one in outs:
        one.wait()
    last.wait()


def shards(n_rep, n_fsdp, tokens, norm_gain, step_counts, local_params, global_params, momentum):
    count, width = tokens.shape
    _, rows, cols = local_params.shape
    part = cols // n_rep
    n_line = n_fsdp // 2
    chunk = min(128, rows // 2)
    n_chunk = rows // chunk
    first = n_chunk // 2 if n_line >= 4 else n_chunk
    lent_rows = max(rows - first * chunk, 128)
    anywhere = pl.BlockSpec(memory_space=pl.ANY)
    dma = pltpu.SemaphoreType.DMA
    return pl.pallas_call(
        functools.partial(kernel, n_rep, n_line, chunk, 32, first),
        out_shape=(
            jax.ShapeDtypeStruct((count, cols), BF16),
            jax.ShapeDtypeStruct((1, rows, cols), BF16),
            jax.ShapeDtypeStruct((rows, part), F32),
            jax.ShapeDtypeStruct((rows, part), F32),
        ),
        in_specs=[
            pl.BlockSpec(memory_space=pltpu.SMEM),
            pl.BlockSpec(memory_space=pltpu.VMEM),
            anywhere, anywhere, anywhere, anywhere,
        ],
        out_specs=(anywhere,) * 4,
        scratch_shapes=[
            pltpu.VMEM((count, width), BF16),
            pltpu.VMEM((n_fsdp, rows, cols), BF16),
            pltpu.VMEM((rows, cols), BF16),
            pltpu.VMEM((rows, part), F32),
            pltpu.VMEM((rows, part), F32),
            pltpu.VMEM((n_rep, rows, part), BF16),
            pltpu.VMEM((n_rep, rows, part), BF16),
            pltpu.VMEM((n_rep, 8, part), F32),
            pltpu.VMEM((count, cols), F32),
            pltpu.VMEM((count, cols), BF16),
            pltpu.VMEM((4, count, lent_rows), BF16),
            pltpu.VMEM((count, cols), BF16),
            pltpu.VMEM((count, cols), BF16),
            dma((4,)), dma((4,)),
            dma((n_rep - 1,)), dma((n_rep - 1,)),
            dma((n_rep - 1, n_chunk)), dma((n_rep - 1, n_chunk)),
            dma((n_rep - 1, n_chunk)), dma((n_rep - 1, n_chunk)),
            dma((n_line, n_chunk)), dma((n_line, n_chunk)), dma((n_line, n_chunk)),
            dma((n_line, n_chunk)), dma((n_line, n_chunk)),
            dma((4,)), dma((4,)), dma((max(cols // 256, 1),)), dma((max(cols // 256, 1),)),
        ],
        compiler_params=pltpu.CompilerParams(
            collective_id=0, has_side_effects=True, vmem_limit_bytes=60 * 2**20
        ),
    )(step_counts, norm_gain.reshape(1, width), tokens, local_params, global_params, momentum)


def solution(mesh):
    return jax.shard_map(
        functools.partial(shards, mesh.shape["rep"], mesh.shape["fsdp"]),
        mesh=mesh,
        in_specs=(
            P(("rep", "fsdp"), None),
            P(),
            P("rep"),
            P("rep", "fsdp", None),
            P("fsdp", "rep"),
            P("fsdp", "rep"),
        ),
        out_specs=(
            P(("rep", "fsdp"), None),
            P("rep", "fsdp", None),
            P("fsdp", "rep"),
            P("fsdp", "rep"),
        ),
        check_vma=False,
    )
```

```python
import functools

import jax
import jax.numpy as jnp
from jax import lax
from jax.experimental import pallas as pl
from jax.experimental.pallas import tpu as pltpu
from jax.sharding import PartitionSpec as P

MESH = pl.DeviceIdType.MESH
BF16 = jnp.bfloat16
F32 = jnp.float32


def kernel(
    n_rep, n_line, chunk, step, first,
    counts, gain, tok_hbm, loc_hbm, glob_hbm, mom_hbm,
    kv_out, nl_out, ng_out, nm_out,
    tok, w, loc, glob, mom, got, ag, cnt, acc, kv, lent, part_out, part_in,
    load_sem, out_sem, cs, cr, rss, rsr, ags, agr, zr, zu, zd, ss, sr, ts, tr, ps, pr,
):
    me = lax.axis_index("rep")
    f = lax.axis_index("fsdp")
    z = f // 2
    core = f % 2
    rows, cols = loc.shape
    part = cols // n_rep
    n_chunk = rows // chunk
    at_end = jnp.logical_or(z == 0, z == n_line - 1)
    helps = jnp.logical_or(z == 1, z == n_line - 2)
    low = z < n_line // 2
    inward = jnp.where(low, f + 2, f - 2)
    outward = jnp.where(low, f - 2, f + 2)
    lend = first < n_chunk

    def lent_out(dest, src, k):
        if not lend:
            return dest < 0
        dist = jnp.where(dest == 0, src, n_line - 1 - src)
        near = jnp.logical_or(dist == 1, dist == 2)
        end = jnp.logical_or(dest == 0, dest == n_line - 1)
        return jnp.logical_and(jnp.logical_and(end, near), k >= first)

    def goes_up(src, k):
        return jnp.logical_and(z < n_line - 1, jnp.logical_not(lent_out(z + 1, src, k)))

    def goes_down(src, k):
        return jnp.logical_and(z > 0, jnp.logical_not(lent_out(z - 1, src, k)))

    def load(i, src, dst):
        return pltpu.make_async_copy(src, dst, load_sem.at[i])

    loads = [
        load(0, loc_hbm.at[0], loc),
        load(1, glob_hbm, glob),
        load(2, mom_hbm, mom),
        load(3, tok_hbm, tok),
    ]
    for one in loads:
        one.start()
    cnt[me] = jnp.full(cnt.shape[1:], counts[0].astype(F32), F32)

    barrier = pltpu.get_barrier_semaphore()
    for j in range(1, n_rep):
        pl.semaphore_signal(barrier, inc=1, device_id={"rep": (me + j) % n_rep}, device_id_type=MESH)
    pl.semaphore_signal(barrier, inc=1, device_id={"fsdp": z * 2 + 1 - core}, device_id_type=MESH)

    @pl.when(z > 0)
    def _():
        pl.semaphore_signal(barrier, inc=1, device_id={"fsdp": f - 2}, device_id_type=MESH)

    @pl.when(z < n_line - 1)
    def _():
        pl.semaphore_signal(barrier, inc=1, device_id={"fsdp": f + 2}, device_id_type=MESH)

    ends = (z == 0).astype(jnp.int32) + (z == n_line - 1).astype(jnp.int32)
    pl.semaphore_wait(barrier, n_rep + 2 - ends)

    def span(k):
        return pl.ds(pl.multiple_of(k * chunk, chunk), chunk)

    def slot(p):
        return pl.ds(pl.multiple_of(p * part, part), part)

    def count_copy(j, owner):
        return pltpu.make_async_remote_copy(
            cnt.at[owner], cnt.at[owner], cs.at[j - 1], cr.at[j - 1],
            device_id={"rep": (me + j) % n_rep}, device_id_type=MESH)

    def part_copy(j, k):
        to = (me + j) % n_rep
        return pltpu.make_async_remote_copy(
            loc.at[span(k), slot(to)], got.at[me, span(k)], rss.at[j - 1, k], rsr.at[j - 1, k],
            device_id={"rep": to}, device_id_type=MESH)

    def part_wait(j, k):
        owner = (me + n_rep - j) % n_rep
        pltpu.make_async_remote_copy(
            got.at[owner, span(k)], got.at[owner, span(k)], rss.at[j - 1, k], rsr.at[j - 1, k],
            device_id={"rep": (me + j) % n_rep}, device_id_type=MESH).wait_recv()

    def new_copy(j, k, owner):
        return pltpu.make_async_remote_copy(
            ag.at[owner, span(k)], ag.at[owner, span(k)], ags.at[j - 1, k], agr.at[j - 1, k],
            device_id={"rep": (me + j) % n_rep}, device_id_type=MESH)

    def line_copy(src, k, up):
        sem = zu if up else zd
        block = w.at[src * 2 + core, span(k)]
        return pltpu.make_async_remote_copy(
            block, block, sem.at[src, k], zr.at[src, k],
            device_id={"fsdp": f + 2 if up else f - 2}, device_id_type=MESH)

    def pair_copy(src, k, owner):
        block = w.at[src * 2 + owner, span(k)]
        return pltpu.make_async_remote_copy(
            block, block, ss.at[src, k], sr.at[src, k],
            device_id={"fsdp": z * 2 + 1 - core}, device_id_type=MESH)

    def send_parts(k):
        for j in range(1, n_rep):
            part_copy(j, k).start()

    def pass_on(src, k, up, down):
        @pl.when(jnp.logical_and(up, goes_up(src, k)))
        def _():
            line_copy(src, k, True).start()

        @pl.when(jnp.logical_and(down, goes_down(src, k)))
        def _():
            line_copy(src, k, False).start()

        pair_copy(src, k, core).start()

    def lent_block(q, low_end):
        d = q // 2 + 1
        return jnp.where(low_end, d, n_line - 1 - d) * 2 + q % 2

    lent_rows = rows - first * chunk

    def lent_copy(q):
        at = pl.multiple_of(lent_block(q, low) * rows + first * chunk, chunk)
        return pltpu.make_async_remote_copy(
            tok.at[:, pl.ds(at, lent_rows)], lent.at[q], ts.at[q], tr.at[q],
            device_id={"fsdp": inward}, device_id_type=MESH)

    wide_cols = min(256, cols)
    n_wide = cols // wide_cols

    def part_back(i):
        c = slice(i * wide_cols, (i + 1) * wide_cols)
        return pltpu.make_async_remote_copy(
            part_out.at[:, c], part_in.at[:, c], ps.at[i], pr.at[i],
            device_id={"fsdp": outward}, device_id_type=MESH)

    def help_end():
        for q in range(4):
            lent_copy(q).wait_recv()
        for i in range(n_wide):
            c = slice(i * wide_cols, (i + 1) * wide_cols)
            summed = jnp.zeros((tok.shape[0], wide_cols), F32)
            for q in range(4):
                summed = summed + jnp.dot(
                    lent[q], w[lent_block(q, low), first * chunk :, c], preferred_element_type=F32)
            part_out[:, c] = summed.astype(BF16)
            part_back(i).start()

    loads[0].wait()
    for j in range(1, n_rep):
        count_copy(j, me).start()
    ahead = min(2, n_chunk)
    for k in range(ahead):
        send_parts(k)
    loads[1].wait()
    loads[2].wait()
    for j in range(1, n_rep):
        count_copy(j, (me + n_rep - j) % n_rep).wait_recv()
    total = cnt[0, 0:1, :]
    for r in range(1, n_rep):
        total = total + cnt[r, 0:1, :]

    def reduce_chunk(k):
        for j in range(1, n_rep):
            part_wait(j, k)

        def some(i, carry):
            at = pl.ds(pl.multiple_of(k * chunk + i * step, step), step)
            summed = cnt[me, 0:1, :] * loc[at, slot(me)].astype(F32)
            for j in range(1, n_rep):
                r = (me + j) % n_rep
                summed = summed + cnt[r, 0:1, :] * got[r, at, :].astype(F32)
            old = glob[at, :]
            delta = old - summed / total
            moment = 0.9 * mom[at, :] + delta
            new = old - 0.7 * (delta + 0.9 * moment)
            mom[at, :] = moment
            glob[at, :] = new
            ag[me, at, :] = new.astype(BF16)
            return carry

        lax.fori_loop(0, chunk // step, some, 0)
        for j in range(1, n_rep):
            new_copy(j, k, me).start()

    def mix_chunk(k):
        for j in range(1, n_rep):
            new_copy(j, k, (me + n_rep - j) % n_rep).wait_recv()

        def some(i, carry):
            at = pl.ds(pl.multiple_of(k * chunk + i * step, step), step)
            for r in range(n_rep):
                c = slice(r * part, (r + 1) * part)
                mixed = 0.5 * loc[at, c].astype(F32) + 0.5 * ag[r, at, :].astype(F32)
                w[f, at, c] = mixed.astype(BF16)
            return carry

        lax.fori_loop(0, chunk // step, some, 0)
        inner = jnp.logical_not(at_end) if lend and k < n_chunk // 2 else True
        pass_on(z, k, inner, inner)

    def norm():
        loads[3].wait()

        def some(i, carry):
            at = pl.ds(pl.multiple_of(i * 16, 16), 16)
            wide = tok[at, :].astype(F32)
            square = jnp.mean(wide * wide, axis=1, keepdims=True)
            tok[at, :] = (wide * lax.rsqrt(square + 1e-05) * gain[...].astype(F32)).astype(BF16)
            return carry

        lax.fori_loop(0, tok.shape[0] // 16, some, 0)
        acc[...] = jnp.zeros_like(acc)

    if lend:
        @pl.when(at_end)
        def _():
            norm()
            for q in range(4):
                lent_copy(q).start()

    def multiply(at, k):
        a = tok[:, pl.ds(pl.multiple_of(at * rows + k * chunk, chunk), chunk)]

        def some(i, carry):
            c = pl.ds(pl.multiple_of(i * wide_cols, wide_cols), wide_cols)
            acc[:, c] += jnp.dot(a, w[at, span(k), c], preferred_element_type=F32)
            return carry

        lax.fori_loop(0, cols // wide_cols, some, 0)

    def compute(src, k):
        multiply(src * 2 + core, k)
        pair_copy(src, k, 1 - core).wait_recv()
        multiply(src * 2 + 1 - core, k)

    def own(k, carry):
        compute(z, k)
        return carry

    base = n_chunk * jnp.maximum(jnp.maximum(z - 1, n_line - 2 - z), 0)

    def arrival(t, up):
        room = z if up else n_line - 1 - z
        early = t < base
        k = jnp.where(early, t % n_chunk, t - base - room)
        dist = jnp.where(early, t // n_chunk + 1, room)
        src = z - dist if up else z + dist
        inside = jnp.where(early, dist < room, room > 0)
        there = jnp.logical_and(inside, jnp.logical_and(k >= 0, k < n_chunk))
        return jnp.logical_and(there, jnp.logical_not(lent_out(z, src, k))), src, k

    def receive(t):
        for up in (True, False):
            there, src, k = arrival(t, up)

            @pl.when(there)
            def _():
                line_copy(src, k, up).wait_recv()
                pass_on(src, k, up, not up)

    def finish(t):
        for up in (True, False):
            there, src, k = arrival(t, up)

            @pl.when(there)
            def _():
                compute(src, k)

    n_event = n_line * n_chunk
    n_tick = (n_line - 2) * n_chunk + n_chunk + n_line
    hold = 1
    for k in range(n_chunk + 1):
        if k < n_chunk:
            reduce_chunk(k)
            if k + ahead < n_chunk:
                send_parts(k + ahead)
        if k == 0:
            if lend:
                pl.when(jnp.logical_not(at_end))(norm)
            else:
                norm()
        if k >= 1:
            if lend and k - 1 == n_chunk // 2:
                @pl.when(z == 0)
                def _():
                    for held in range(n_chunk // 2):
                        line_copy(z, held, True).start()

                @pl.when(z == n_line - 1)
                def _():
                    for held in range(n_chunk // 2):
                        line_copy(z, held, False).start()

            mix_chunk(k - 1)
        if k >= 1 + hold:
            t = k - 1 - hold
            receive(t)
            own(t, 0)
            if t >= 1:
                finish(t - 1)
    caught = n_chunk - hold

    outs = [
        pltpu.make_async_copy(glob, ng_out, out_sem.at[0]),
        pltpu.make_async_copy(mom, nm_out, out_sem.at[1]),
        pltpu.make_async_copy(w.at[f], nl_out.at[0], out_sem.at[2]),
    ]
    for one in outs:
        one.start()

    receive(caught)
    if caught >= 1:
        finish(caught - 1)
    for k in range(caught, n_chunk):
        own(k, 0)

    def later(t, carry):
        receive(t)
        finish(t - 1)
        if lend:
            @pl.when(jnp.logical_and(helps, t == base))
            def _():
                help_end()
        return carry

    lax.fori_loop(caught + 1, n_tick + 1, later, 0)

    scale = (n_line * 2 * rows) ** (-0.5)

    def scaled(i, carry):
        at = pl.ds(pl.multiple_of(i * 64, 64), 64)
        kv[at, :] = (acc[at, :] * scale).astype(BF16)
        return carry

    if lend:
        @pl.when(at_end)
        def _():
            for q in range(4):
                lent_copy(q).wait_send()
            for i in range(n_wide):
                part_back(i).wait_recv()

            def add(i, carry):
                at = pl.ds(pl.multiple_of(i * 64, 64), 64)
                acc[at, :] += part_in[at, :].astype(F32)
                return carry

            lax.fori_loop(0, acc.shape[0] // 64, add, 0)

        @pl.when(helps)
        def _():
            for i in range(n_wide):
                part_back(i).wait_send()

    lax.fori_loop(0, acc.shape[0] // 64, scaled, 0)
    last = pltpu.make_async_copy(kv, kv_out, out_sem.at[3])
    last.start()

    for j in range(1, n_rep):
        count_copy(j, me).wait_send()

    def sent(k, carry):
        for j in range(1, n_rep):
            part_copy(j, k).wait_send()
            new_copy(j, k, me).wait_send()
        return carry

    lax.fori_loop(0, n_chunk, sent, 0)

    def passed(t, carry):
        src = t // n_chunk
        k = t % n_chunk

        @pl.when(jnp.logical_and(src <= z, goes_up(src, k)))
        def _():
            line_copy(src, k, True).wait_send()

        @pl.when(jnp.logical_and(src >= z, goes_down(src, k)))
        def _():
            line_copy(src, k, False).wait_send()

        @pl.when(jnp.logical_not(lent_out(z, src, k)))
        def _():
            pair_copy(src, k, core).wait_send()
        return carry

    lax.fori_loop(0, n_event, passed, 0)
    for one in outs:
        one.wait()
    last.wait()


def shards(n_rep, n_fsdp, tokens, norm_gain, step_counts, local_params, global_params, momentum):
    count, width = tokens.shape
    _, rows, cols = local_params.shape
    part = cols // n_rep
    n_line = n_fsdp // 2
    chunk = min(128, rows // 2)
    n_chunk = rows // chunk
    first = n_chunk // 2 if n_line >= 4 else n_chunk
    lent_rows = max(rows - first * chunk, 128)
    anywhere = pl.BlockSpec(memory_space=pl.ANY)
    dma = pltpu.SemaphoreType.DMA
    return pl.pallas_call(
        functools.partial(kernel, n_rep, n_line, chunk, 32, first),
        out_shape=(
            jax.ShapeDtypeStruct((count, cols), BF16),
            jax.ShapeDtypeStruct((1, rows, cols), BF16),
            jax.ShapeDtypeStruct((rows, part), F32),
            jax.ShapeDtypeStruct((rows, part), F32),
        ),
        in_specs=[
            pl.BlockSpec(memory_space=pltpu.SMEM),
            pl.BlockSpec(memory_space=pltpu.VMEM),
            anywhere, anywhere, anywhere, anywhere,
        ],
        out_specs=(anywhere,) * 4,
        scratch_shapes=[
            pltpu.VMEM((count, width), BF16),
            pltpu.VMEM((n_fsdp, rows, cols), BF16),
            pltpu.VMEM((rows, cols), BF16),
            pltpu.VMEM((rows, part), F32),
            pltpu.VMEM((rows, part), F32),
            pltpu.VMEM((n_rep, rows, part), BF16),
            pltpu.VMEM((n_rep, rows, part), BF16),
            pltpu.VMEM((n_rep, 8, part), F32),
            pltpu.VMEM((count, cols), F32),
            pltpu.VMEM((count, cols), BF16),
            pltpu.VMEM((4, count, lent_rows), BF16),
            pltpu.VMEM((count, cols), BF16),
            pltpu.VMEM((count, cols), BF16),
            dma((4,)), dma((4,)),
            dma((n_rep - 1,)), dma((n_rep - 1,)),
            dma((n_rep - 1, n_chunk)), dma((n_rep - 1, n_chunk)),
            dma((n_rep - 1, n_chunk)), dma((n_rep - 1, n_chunk)),
            dma((n_line, n_chunk)), dma((n_line, n_chunk)), dma((n_line, n_chunk)),
            dma((n_line, n_chunk)), dma((n_line, n_chunk)),
            dma((4,)), dma((4,)), dma((max(cols // 256, 1),)), dma((max(cols // 256, 1),)),
        ],
        compiler_params=pltpu.CompilerParams(
            collective_id=0, has_side_effects=True, vmem_limit_bytes=60 * 2**20
        ),
    )(step_counts, norm_gain.reshape(1, width), tokens, local_params, global_params, momentum)


def solution(mesh):
    return jax.shard_map(
        functools.partial(shards, mesh.shape["rep"], mesh.shape["fsdp"]),
        mesh=mesh,
        in_specs=(
            P(("rep", "fsdp"), None),
            P(),
            P("rep"),
            P("rep", "fsdp", None),
            P("fsdp", "rep"),
            P("fsdp", "rep"),
        ),
        out_specs=(
            P(("rep", "fsdp"), None),
            P("rep", "fsdp", None),
            P("fsdp", "rep"),
            P("fsdp", "rep"),
        ),
        check_vma=False,
    )
```
